32 devices in a mesh: out: 8 (over y, x, core), in: 4 (over z).
Axes of the slice: x: 2, y: 2, z: 4, core: 2. Of those that a mesh axis runs over, the one named last changes fastest.
Arguments:
- activations: bfloat16 [512, 8192], P('in', 'out'), may hold values from -6 to 6
- out_grad: bfloat16 [512, 28672], P('out', 'in'), may hold values from -6 to 6
- basis_out: bfloat16 [28672, 28672], P('in', 'out'), may hold values from -0.03125 to 0.03125
- basis_in: bfloat16 [8192, 8192], P('out', 'in'), may hold values from -0.0625 to 0.0625
- eigenvalues: bfloat16 [28672, 8192], P('out', 'in'), may hold values from 0.5 to 8
- query_out: bfloat16 [256, 28672], P(None, 'in'), may hold values from -0.0078125 to 0.0078125
- query_in: bfloat16 [256, 8192], P(None, 'out'), may hold values from -0.015625 to 0.015625
- query_domain: int32 [32], replicated, may hold values from 0 to 7
- seq_weight: int32 [4, 8], replicated, may hold values from 1 to 16
Outputs:
- mixed: bfloat16 [28672, 8192], P('out', 'in')
- influence: float32 [4, 32], replicated
The draws below stay inside these ranges and needn't reach their ends.
All inputs are finite; a program needn't handle non-finite values.
Results may differ from the reference program's by a relative error of at most 0.0065.
Values may be sent and summed in bfloat16 or wider, within the bound.
No kernel may reach another device: no remote copies, remote signals or barrier semaphores. Data moves between devices by JAX's collectives and lax.ppermute only.
A program may use at most 256 MiB of HBM per device.

```python
import math
import jax
import jax.numpy as jnp
from jax import lax

D = 8192
FF = 28672
SEQS = 4
LEN = 128
QUERIES = 32
RANK = 8
DOMAINS = 8
TOKENS = 512
QROWS = 256


def place_ends(entries, key, least, largest):
    longest = entries.shape.index(max(entries.shape))
    spots = []
    for shift in (0, 1):
        where = [jax.random.randint(jax.random.fold_in(key, axis), (), 0, length) for axis, length in enumerate(entries.shape)]
        where[longest] = (where[longest] + shift) % entries.shape[longest]
        spots.append(tuple(where))
    return entries.at[spots[0]].set(least).at[spots[1]].set(largest)


def block_scale(stream_key, dims, split, least, high):
    gain, own = 1.0, jax.random.fold_in(stream_key, 6)
    for position, blocks in split:
        draws = jnp.exp(jax.random.uniform(jax.random.fold_in(own, position), (blocks,), jnp.float32, least / len(split), high / len(split)))
        gain = gain * jnp.repeat(draws, dims[position] // blocks).reshape([-1 if axis == position else 1 for axis in range(len(dims))])
    return gain


def noise(key, shape, width, limit, cuts=(), kind=jnp.bfloat16):
    drawn = width * jax.random.normal(key, shape, jnp.float32)
    if cuts:
        drawn = drawn * block_scale(key, shape, cuts, -0.22, 0.18)
    return jnp.clip(drawn, -limit, limit).astype(kind)


def setup_inputs(seed: int = 0) -> dict:
    splits = jax.random.split(jax.random.key(seed), 10)
    activations = noise(splits[0], (TOKENS, D), 1.0, 6.0, ((0, 4), (1, 8)))
    out_grad = noise(splits[1], (TOKENS, FF), 1.0, 6.0, ((0, 8), (1, 4)))
    basis_out = noise(splits[2], (FF, FF), FF ** -0.5, 0.03125, ((0, 4), (1, 8)))
    basis_in = noise(splits[3], (D, D), D ** -0.5, 0.0625, ((0, 8), (1, 4)))
    eigenvalues = jnp.clip(jnp.exp(math.log(8.0) - 2.7725887 * jax.random.uniform(splits[4], (FF, D), jnp.float32) ** block_scale(splits[4], (FF, D), ((0, 8), (1, 4)), -0.2, 0.2)), 0.5, 8.0).astype(jnp.bfloat16)
    query_out = noise(splits[5], (QROWS, FF), (FF * 16) ** -0.5, 0.0078125, ((1, 4),))
    query_in = noise(splits[6], (QROWS, D), (D * 16) ** -0.5, 0.015625, ((1, 8),))
    query_domain = place_ends(jax.random.randint(splits[7], (QUERIES,), 0, DOMAINS), jax.random.fold_in(splits[7], 1), 0, DOMAINS - 1).astype(jnp.int32)
    seq_weight = place_ends(jax.random.randint(splits[8], (SEQS, DOMAINS), 1, 17), jax.random.fold_in(splits[8], 1), 1, 16).astype(jnp.int32)
    return dict(activations=activations, out_grad=out_grad, basis_out=basis_out, basis_in=basis_in, eigenvalues=eigenvalues, query_out=query_out, query_in=query_in, query_domain=query_domain, seq_weight=seq_weight)


def reference(activations, out_grad, basis_out, basis_in, eigenvalues, query_out, query_in, query_domain, seq_weight):
    rot_grad = jnp.dot(out_grad, basis_out, preferred_element_type=jnp.float32).astype(jnp.bfloat16)
    rot_act = jnp.dot(activations, basis_in, preferred_element_type=jnp.float32).astype(jnp.bfloat16)
    rot_qout = jnp.dot(query_out, basis_out, preferred_element_type=jnp.float32).astype(jnp.bfloat16)
    rot_qin = jnp.dot(query_in, basis_in, preferred_element_type=jnp.float32).astype(jnp.bfloat16)
    eigen_full = eigenvalues.astype(jnp.float32)
    qout_float = rot_qout.astype(jnp.float32)
    accumulated = jnp.zeros((FF, D), jnp.float32)
    partials = []
    for sequence in range(SEQS):
        lower = sequence * LEN
        grad_block = rot_grad[lower:lower + LEN]
        act_block = rot_act[lower:lower + LEN]
        rotated = lax.dot_general(grad_block, act_block, (((0,), (0,)), ((), ())), preferred_element_type=jnp.float32)
        precond = rotated / eigen_full
        accumulated = accumulated + precond
        projected = lax.dot_general(rot_qin, precond.astype(jnp.bfloat16), (((1,), (1,)), ((), ())), preferred_element_type=jnp.float32)
        per_factor = lax.optimization_barrier(jnp.sum(projected * qout_float, axis=1))
        partials.append(lax.optimization_barrier(jnp.sum(per_factor.reshape(QUERIES, RANK), axis=1)))
    score = jnp.stack(partials)
    mixed = (accumulated * (1.0 / math.sqrt(SEQS * LEN))).astype(jnp.bfloat16)
    weights = seq_weight.astype(jnp.float32)
    onehot = (query_domain[:, None] == jnp.arange(DOMAINS, dtype=jnp.int32)[None, :]).astype(jnp.float32)
    picked = lax.optimization_barrier(jnp.sum(weights[:, None, :] * onehot[None, :, :], axis=2))
    mean_weight = lax.optimization_barrier(jnp.sum(weights, axis=1, keepdims=True)) / DOMAINS
    influence = score * picked / mean_weight
    return (mixed, influence)
```

```python
import functools
import math

import jax
import jax.numpy as jnp
from jax import lax
from jax.experimental import pallas as pl
from jax.experimental.pallas import tpu as pltpu
from jax.sharding import PartitionSpec as P

SEQS = 4
RANK = 8
DOMAINS = 8
LAG = 2
F32 = jnp.float32
BF16 = jnp.bfloat16
ANY = pl.BlockSpec(memory_space=pl.ANY)
SMEM = pl.BlockSpec(memory_space=pltpu.SMEM)
MIB = 1024 * 1024


def swap(x, axis, size, bit):
    return lax.ppermute(x, axis, [(i, i ^ bit) for i in range(size)])


def tile_of(width, most):
    best = 128
    for tile in range(128, most + 1, 128):
        if width % tile == 0:
            best = tile
    return best


def cost(flops, moved):
    return pl.CostEstimate(flops=flops, bytes_accessed=moved, transcendentals=0)


class Order:
    def __init__(self):
        self.last = []

    def call(self, body, operands, specs, out_specs, out_shape, room=48, **options):
        count, extra, outs = len(operands), len(self.last), len(out_shape)

        def wrapped(*refs):
            ends = refs[count + extra :]
            body(*refs[:count], *ends[:outs], *ends[outs + 1 :])
            ends[outs][...] = jnp.zeros_like(ends[outs])

        *results, mark = pl.pallas_call(
            wrapped,
            in_specs=specs + [ANY] * extra,
            out_specs=list(out_specs) + [pl.BlockSpec((8, 128), lambda i: (0, 0))],
            out_shape=list(out_shape) + [jax.ShapeDtypeStruct((8, 128), F32)],
            compiler_params=pltpu.CompilerParams(vmem_limit_bytes=room * MIB),
            **options,
        )(*operands, *self.last)
        self.last = [mark]
        return results


def rotate_down(order, rows, basis, unit, first, count):
    height, depth = rows.shape
    blocks = basis.shape[1] // unit

    def body(rows_ref, basis_ref, out_ref):
        real = first + pl.program_id(0) < blocks

        @pl.when(real)
        def _():
            out_ref[...] = jnp.dot(
                rows_ref[...], basis_ref[...], preferred_element_type=F32
            ).astype(BF16)

        @pl.when(jnp.logical_not(real))
        def _():
            out_ref[...] = jnp.zeros_like(out_ref)

    return order.call(
        body,
        [rows, basis],
        [
            pl.BlockSpec((height, depth), lambda i: (0, 0), pipeline_mode=pl.Buffered(1)),
            pl.BlockSpec((depth, unit), lambda i: (0, jnp.minimum(first + i, blocks - 1))),
        ],
        grid=(count,),
        out_specs=[pl.BlockSpec((height, unit), lambda i: (i, 0))],
        out_shape=[jax.ShapeDtypeStruct((height * count, unit), BF16)],
        cost_estimate=cost(2 * height * depth * unit * count, 2 * depth * unit * count),
    )[0]


def rotate_pieces(order, pieces, offsets, tokens, basis, lower, width, most):
    depth = basis.shape[0]
    tile = tile_of(math.gcd(width, lower) if lower else width, most)
    first = lower // tile
    count = len(pieces)

    def body(offsets_ref, *refs):
        held, (basis_ref, out_ref, rows_ref, sems) = refs[:count], refs[count:]

        @pl.when(pl.program_id(0) == 0)
        def _():
            copies = []
            for n, piece in enumerate(held):
                size = piece.shape[0]
                where = pl.multiple_of(offsets_ref[n] * size, size)
                copies.append(
                    pltpu.make_async_copy(piece, rows_ref.at[pl.ds(where, size), :], sems.at[n])
                )
            for copy in copies:
                copy.start()
            for copy in copies:
                copy.wait()

        out_ref[...] = jnp.dot(rows_ref[...], basis_ref[...], preferred_element_type=F32).astype(
            BF16
        )

    return order.call(
        body,
        [offsets, *pieces, basis],
        [SMEM] + [ANY] * count + [pl.BlockSpec((depth, tile), lambda i: (0, first + i))],
        grid=(width // tile,),
        out_specs=[pl.BlockSpec((tokens, tile), lambda i: (0, i))],
        out_shape=[jax.ShapeDtypeStruct((tokens, width), BF16)],
        scratch_shapes=[
            pltpu.VMEM((tokens, depth), BF16),
            pltpu.SemaphoreType.DMA((count,)),
        ],
        cost_estimate=cost(2 * tokens * depth * width, 2 * depth * width),
    )[0]


def pick(place, groups):
    result = groups[0][1]
    for places, value in groups[1:]:
        here = functools.reduce(jnp.logical_or, [place == p for p in places])
        result = jnp.where(here, value, result)
    return result


class Line:
    def __init__(self, axis, size, place, shape, count):
        self.axis, self.size, self.place = axis, size, place
        self.shape, self.count = shape, count
        self.parts = []
        self.got = [{}, {}]

    def step(self, order, s):
        size, (rows, columns) = self.size, self.shape
        halves = 2
        block = (rows // halves, columns)
        plan, operands, specs = [], [self.place], [SMEM]
        for parity in (0, 1):
            groups = {}
            for place in range(size):
                if parity == 1 and place in (0, size - 1):
                    continue
                chunk = s - LAG * (place if place % 2 == parity else size - 1 - place)
                if 0 <= chunk < self.count:
                    groups.setdefault(chunk, []).append(place)
            if not groups:
                continue
            for chunk in groups:
                array, row, column = self.parts[chunk]
                operands.append(array)
                specs.append(
                    pl.BlockSpec(block, lambda i, r=row, c=column: (r * halves + i, c))
                )
            before = self.got[1 - parity].get(s - LAG)
            if before is not None:
                operands.append(before)
                specs.append(pl.BlockSpec(block, lambda i: (i, 0)))
            plan.append((parity, list(groups.values()), before is not None))
        outs = len(plan)

        def body(place_ref, *refs):
            place = place_ref[0]
            loads, refs = refs[len(refs) - outs :], iter(refs)
            for (_, groups, more), load in zip(plan, loads):
                value = pick(place, [(places, next(refs)[...]) for places in groups])
                if more:
                    value = (value.astype(F32) + next(refs)[...].astype(F32)).astype(BF16)
                load[...] = value

        loads = order.call(
            body,
            operands,
            specs,
            grid=(halves,),
            out_specs=[pl.BlockSpec(block, lambda i: (i, 0))] * outs,
            out_shape=[jax.ShapeDtypeStruct(self.shape, BF16)] * outs,
            cost_estimate=cost(rows * columns * 4, 2 * rows * columns * (len(operands) + outs)),
        )
        for (parity, _, _), load in zip(plan, loads):
            pairs = []
            for place in range(parity, size - 1, 2):
                pairs += [(place, place + 1), (place + 1, place)]
            self.got[parity][s] = lax.ppermute(load, self.axis, pairs)

    def terms(self, chunk):
        groups = {}
        for place in range(self.size):
            keys = []
            if place > 0:
                keys.append(((place - 1) % 2, place - 1))
            if place < self.size - 1:
                keys.append((place % 2, self.size - 2 - place))
            groups.setdefault(tuple(sorted(keys)), []).append(place)
        return [
            (places, [self.got[parity][chunk + LAG * late] for parity, late in keys])
            for keys, places in groups.items()
        ]


def score(order, line, chunk, query_chunk, query_row, act, qin_turned, eigen, mixed, first, queries):
    tokens, inner = act.shape
    unit = line.shape[1]
    tile = tile_of(unit, 256)
    tiles = unit // tile
    step = tile_of(inner, 256)
    length = tokens // SEQS
    gain = 1.0 / math.sqrt(tokens)
    operands, specs, plan = [line.place], [SMEM], []
    share = line.shape[0] // queries
    for number, row, height in ((chunk, 0, tokens), (query_chunk, query_row, queries)):
        array, low, column = line.parts[number]
        low = low * (share if height == queries else 1) + row
        operands.append(array)
        specs.append(
            pl.BlockSpec((height, tile), lambda i, r=low, c=column: (r, c * tiles + i))
        )
        groups = []
        for places, arrays in line.terms(number):
            for array in arrays:
                operands.append(array)
                specs.append(pl.BlockSpec((height, tile), lambda i, r=row: (r, i)))
            groups.append((places, len(arrays)))
        plan.append(groups)
    operands += [act, qin_turned, eigen]
    specs += [
        pl.BlockSpec((tokens, inner), lambda i: (0, 0)),
        pl.BlockSpec((inner, queries), lambda i: (0, 0)),
        pl.BlockSpec((tile, inner), lambda i: (first * tiles + i, 0)),
    ]
    aliases = {}
    if mixed is not None:
        aliases = {len(operands): 0}
        operands.append(mixed)
        specs.append(ANY)

    def body(place_ref, *refs):
        place = place_ref[0]
        mixed_ref, score_ref, half_ref = refs[-3:]
        refs = iter(refs)
        totals = []
        for groups in plan:
            own = next(refs)[...].astype(F32)
            sums = []
            for places, number in groups:
                values = [next(refs)[...].astype(F32) for _ in range(number)]
                sums.append((places, functools.reduce(jnp.add, values)))
            totals.append((own + pick(place, sums)).astype(BF16))
        act_ref, qin_ref, eigen_ref = next(refs), next(refs), next(refs)
        turned = jnp.transpose(totals[0])
        for lower in range(0, inner, step):
            span = slice(lower, lower + step)
            inverse = 1.0 / eigen_ref[:, span].astype(F32)
            total = None
            for s in range(SEQS):
                rows = slice(s * length, (s + 1) * length)
                grad = jnp.dot(turned[:, rows], act_ref[rows, span], preferred_element_type=F32)
                precond = grad * inverse
                total = precond if total is None else total + precond
                half_ref[s * tile : (s + 1) * tile, span] = precond.astype(BF16)
            mixed_ref[:, span] = (total * gain).astype(BF16)
        projected = jnp.dot(half_ref[...], qin_ref[...], preferred_element_type=F32)
        qout = jnp.transpose(totals[1]).astype(F32)

        @pl.when(pl.program_id(0) == 0)
        def _():
            score_ref[...] = jnp.zeros_like(score_ref)

        for s in range(SEQS):
            part = projected[s * tile : (s + 1) * tile] * qout
            score_ref[s : s + 1, :] += jnp.sum(part, axis=0, keepdims=True)

    return order.call(
        body,
        operands,
        specs,
        grid=(tiles,),
        out_specs=[
            pl.BlockSpec((tile, inner), lambda i: (first * tiles + i, 0)),
            pl.BlockSpec((SEQS, queries), lambda i: (0, 0)),
        ],
        out_shape=[
            jax.ShapeDtypeStruct(eigen.shape, BF16),
            jax.ShapeDtypeStruct((SEQS, queries), F32),
        ],
        scratch_shapes=[pltpu.VMEM((SEQS * tile, inner), BF16)],
        input_output_aliases=aliases,
        cost_estimate=cost(
            2 * unit * inner * (tokens * 2 + SEQS * queries), 4 * unit * inner
        ),
    )


class Gather:
    def __init__(self, own, outs):
        self.own, self.outs = own, outs
        self.index = lax.axis_index("out")
        self.bits = []
        bit = 2
        while bit < outs:
            self.bits.append(bit)
            bit *= 2
        low, high = self.bits[:2]
        self.near = [swap(own, "out", outs, low), swap(own, "out", outs, high)]
        self.pieces = [(own, self.index), self.moved((own, self.index), 1)]

    def moved(self, piece, bit):
        x, offset = piece
        rows = self.own.shape[0]
        return swap(x, "out", self.outs, bit), offset ^ (bit * (rows // x.shape[0]))

    def spread(self, order):
        rows, depth = self.own.shape
        half = rows // 2
        low, high = self.bits[:2]
        one, two = self.near

        def body(one_ref, two_ref, below_ref, above_ref):
            below_ref[...] = one_ref[...]
            above_ref[...] = two_ref[...]

        below, above = order.call(
            body,
            [one, two],
            [
                pl.BlockSpec((half, depth), lambda i: (1, 0)),
                pl.BlockSpec((half, depth), lambda i: (0, 0)),
            ],
            grid=(1,),
            out_specs=[pl.BlockSpec((half, depth), lambda i: (0, 0))] * 2,
            out_shape=[jax.ShapeDtypeStruct((half, depth), BF16)] * 2,
            cost_estimate=cost(half * depth, 8 * half * depth),
        )
        far = (self.index ^ (low | high)) * 2
        late = [
            (one, self.index ^ low),
            (two, self.index ^ high),
            (swap(above, "out", self.outs, low), far),
            (swap(below, "out", self.outs, high), far + 1),
        ]
        self.pieces += late + [self.moved(piece, 1) for piece in late]
        for bit in self.bits[2:]:
            self.pieces += [self.moved(piece, bit) for piece in self.pieces]
        offsets = jnp.stack([offset for _, offset in self.pieces]).astype(jnp.int32)
        return [x for x, _ in self.pieces], offsets


class SumOut:
    def __init__(self, outs, core):
        self.outs, self.core = outs, core
        self.bits = []
        bit = 2
        while bit < outs:
            self.bits.append(bit)
            bit *= 2

    def start(self, order, rows, more, basis, tile):
        (tokens, depth), extra = rows.shape, more.shape[0]
        half = (tokens + extra) // 2
        width = basis.shape[1]

        def body(core_ref, rows_ref, more_ref, basis_ref, keep_ref, give_ref, all_ref):
            @pl.when(pl.program_id(0) == 0)
            def _():
                all_ref[:tokens] = rows_ref[...]
                all_ref[tokens:] = more_ref[...]

            for ref, side in ((keep_ref, core_ref[0]), (give_ref, 1 - core_ref[0])):
                at = pl.multiple_of(side * half, half)
                ref[...] = jnp.dot(
                    all_ref[pl.ds(at, half), :], basis_ref[...], preferred_element_type=F32
                ).astype(ref.dtype)

        self.keep, give = order.call(
            body,
            [self.core, rows, more, basis],
            [
                SMEM,
                pl.BlockSpec((tokens, depth), lambda i: (0, 0)),
                pl.BlockSpec((extra, depth), lambda i: (0, 0)),
                pl.BlockSpec((depth, tile), lambda i: (0, i)),
            ],
            grid=(width // tile,),
            out_specs=[pl.BlockSpec((half, tile), lambda i: (0, i))] * 2,
            out_shape=[
                jax.ShapeDtypeStruct((half, width), F32),
                jax.ShapeDtypeStruct((half, width), BF16),
            ],
            scratch_shapes=[pltpu.VMEM((tokens + extra, depth), BF16)],
            cost_estimate=cost(4 * half * depth * width, 2 * depth * width),
        )
        self.got = swap(give, "out", self.outs, 1)
        self.stage, self.done = 0, False

    def pieces(self):
        half = self.keep.shape[0]
        return half // 2, self.keep.shape[1]

    def advance(self, order):
        piece, width = self.pieces()
        grid = 2
        block = (piece // grid, width)
        done = self.stage == len(self.bits)
        if self.stage == 0:
            operands = [self.keep, self.keep, self.got, self.got]
            specs = [pl.BlockSpec(block, lambda i, n=n: (n * grid + i, 0)) for n in (0, 1, 0, 1)]
        else:
            operands = list(self.held) + list(self.got)
            specs = [pl.BlockSpec(block, lambda i: (i, 0))] * 4

        def body(low, high, low_more, high_more, *outs):
            for n, (a, b) in enumerate(((low, low_more), (high, high_more))):
                value = a[...] + b[...].astype(F32)
                if done:
                    outs[0][n] = value.astype(BF16)
                else:
                    outs[n][...] = value.astype(BF16)
                    outs[2 + n][...] = value

        if done:
            out_specs = [pl.BlockSpec((2,) + block, lambda i: (0, i, 0))]
            out_shape = [jax.ShapeDtypeStruct((2, piece, width), BF16)]
        else:
            out_specs = [pl.BlockSpec(block, lambda i: (i, 0))] * 4
            out_shape = [
                jax.ShapeDtypeStruct((piece, width), kind) for kind in (BF16, BF16, F32, F32)
            ]
        outs = order.call(
            body,
            operands,
            specs,
            grid=(grid,),
            out_specs=out_specs,
            out_shape=out_shape,
            cost_estimate=cost(2 * piece * width, 12 * piece * width),
        )
        if done:
            self.mine = outs[0].reshape(2 * piece, width)
            self.other = swap(self.mine, "out", self.outs, 1)
            self.done = True
            return
        self.held = outs[2:]
        self.got = [
            swap(outs[0], "out", self.outs, self.bits[self.stage]),
            swap(outs[1], "out", self.outs, self.bits[-1 - self.stage]),
        ]
        self.stage += 1

    def finish(self, order, tokens):
        half, width = self.mine.shape
        extra = 2 * half - tokens

        def body(core_ref, mine_ref, other_ref, act_ref, turned_ref):
            first = core_ref[0] == 0
            top = jnp.where(first, mine_ref[...], other_ref[...])
            bottom = jnp.where(first, other_ref[...], mine_ref[...])
            act_ref[:half] = top
            act_ref[half:] = bottom[: tokens - half]
            turned_ref[...] = jnp.transpose(bottom[tokens - half :])

        tile = tile_of(width, 512)
        return order.call(
            body,
            [self.core, self.mine, self.other],
            [SMEM] + [pl.BlockSpec((half, tile), lambda i: (0, i))] * 2,
            grid=(width // tile,),
            out_specs=[
                pl.BlockSpec((tokens, tile), lambda i: (0, i)),
                pl.BlockSpec((tile, extra), lambda i: (i, 0)),
            ],
            out_shape=[
                jax.ShapeDtypeStruct((tokens, width), BF16),
                jax.ShapeDtypeStruct((width, extra), BF16),
            ],
            cost_estimate=cost(2 * half * width, 8 * half * width),
        )


def on_device(
    outs,
    ins,
    activations,
    out_grad,
    basis_out,
    basis_in,
    eigenvalues,
    query_out,
    query_in,
    query_domain,
    seq_weight,
):
    tokens = activations.shape[0] * ins
    queries = query_out.shape[0]
    columns = basis_out.shape[1]
    inner = basis_in.shape[1]
    order = Order()

    act_rows = lax.all_gather(activations, "in", axis=0, tiled=True)
    gather = Gather(out_grad, outs)
    core = (lax.axis_index("out") & 1).astype(jnp.int32).reshape(1)

    unit = tile_of(columns, 512)
    spans = columns // unit
    share = tokens // queries
    ahead = -(-spans // share)
    place = lax.axis_index("in").astype(jnp.int32).reshape(1)
    line = Line("in", ins, place, (tokens, unit), ahead + spans)

    def queries_part(first, count):
        part = rotate_down(order, query_out, basis_out, unit, first * share, count * share)
        line.parts += [(part, c, 0) for c in range(count)]

    def grads_part(first, count):
        part = rotate_pieces(
            order, *gathered, tokens, basis_out, first * unit, count * unit, 256
        )
        line.parts += [(part, 0, c) for c in range(count)]

    mixed, scores = None, []

    def score_part(g):
        nonlocal mixed
        mixed, part = score(
            order,
            line,
            ahead + g,
            g // share,
            g % share,
            rot_act,
            qin_turned,
            eigenvalues,
            mixed,
            g,
            queries,
        )
        scores.append(part)

    late = LAG * (ins - 2)
    last = ahead + spans - 1 + late
    gathered = rot_act = qin_turned = None
    total = SumOut(outs, core)
    plan = {2: 2, 4: 2, 6: spans}
    made = 0
    for s in range(last + 1):
        if s == 0:
            queries_part(0, 1)
        elif made < spans and s >= ahead + made:
            grads_part(made, 1)
            made += 1
        line.step(order, s)
        target = s - 1 - late - ahead
        if s == 0 and ahead > 1:
            queries_part(1, ahead - 1)
        elif s == 1:
            gathered = gather.spread(order)
        elif s == 2:
            total.start(order, act_rows, query_in, basis_in, tile_of(inner, 512))
        while rot_act is None and s >= 3 and (s % 2 == 1 or s > 7 or target >= 0):
            if not total.done:
                total.advance(order)
            else:
                rot_act, qin_turned = total.finish(order, tokens)
            if target < 0:
                break
        count = min(plan.get(s, 0), spans - made)
        if count > 0:
            grads_part(made, count)
            made += count
        if 0 <= target < spans:
            score_part(target)
    while len(scores) < spans:
        score_part(len(scores))

    scores = functools.reduce(jnp.add, scores)
    for axis, size in (("out", outs), ("in", ins)):
        bit = 1
        while bit < size:
            scores = scores + swap(scores, axis, size, bit)
            bit *= 2
    summed = jnp.sum(scores.reshape(SEQS, queries // RANK, RANK), axis=2)
    weights = seq_weight.astype(F32)
    onehot = (query_domain[:, None] == jnp.arange(DOMAINS, dtype=jnp.int32)[None, :]).astype(F32)
    picked = jnp.sum(weights[:, None, :] * onehot[None, :, :], axis=2)
    mean_weight = jnp.sum(weights, axis=1, keepdims=True) / DOMAINS
    return (mixed, summed * picked / mean_weight)


def solution(mesh):
    return jax.shard_map(
        functools.partial(on_device, mesh.shape["out"], mesh.shape["in"]),
        mesh=mesh,
        in_specs=(
            P("in", "out"),
            P("out", "in"),
            P("in", "out"),
            P("out", "in"),
            P("out", "in"),
            P(None, "in"),
            P(None, "out"),
            P(),
            P(),
        ),
        out_specs=(P("out", "in"), P()),
        check_vma=False,
    )
```

```python
import functools
import math

import jax
import jax.numpy as jnp
from jax import lax
from jax.experimental import pallas as pl
from jax.experimental.pallas import tpu as pltpu
from jax.sharding import PartitionSpec as P

SEQS = 4
RANK = 8
DOMAINS = 8
LAG = 2
F32 = jnp.float32
BF16 = jnp.bfloat16
ANY = pl.BlockSpec(memory_space=pl.ANY)
SMEM = pl.BlockSpec(memory_space=pltpu.SMEM)
MIB = 1024 * 1024


def swap(x, axis, size, bit):
    return lax.ppermute(x, axis, [(i, i ^ bit) for i in range(size)])


def tile_of(width, most):
    best = 128
    for tile in range(128, most + 1, 128):
        if width % tile == 0:
            best = tile
    return best


def cost(flops, moved):
    return pl.CostEstimate(flops=flops, bytes_accessed=moved, transcendentals=0)


class Order:
    def __init__(self):
        self.last = []

    def call(self, body, operands, specs, out_specs, out_shape, room=48, **options):
        count, extra, outs = len(operands), len(self.last), len(out_shape)

        def wrapped(*refs):
            ends = refs[count + extra :]
            body(*refs[:count], *ends[:outs], *ends[outs + 1 :])
            ends[outs][...] = jnp.zeros_like(ends[outs])

        *results, mark = pl.pallas_call(
            wrapped,
            in_specs=specs + [ANY] * extra,
            out_specs=list(out_specs) + [pl.BlockSpec((8, 128), lambda i: (0, 0))],
            out_shape=list(out_shape) + [jax.ShapeDtypeStruct((8, 128), F32)],
            compiler_params=pltpu.CompilerParams(vmem_limit_bytes=room * MIB),
            **options,
        )(*operands, *self.last)
        self.last = [mark]
        return results


def rotate_down(order, rows, basis, unit, first, count):
    height, depth = rows.shape
    blocks = basis.shape[1] // unit

    def body(rows_ref, basis_ref, out_ref):
        real = first + pl.program_id(0) < blocks

        @pl.when(real)
        def _():
            out_ref[...] = jnp.dot(
                rows_ref[...], basis_ref[...], preferred_element_type=F32
            ).astype(BF16)

        @pl.when(jnp.logical_not(real))
        def _():
            out_ref[...] = jnp.zeros_like(out_ref)

    return order.call(
        body,
        [rows, basis],
        [
            pl.BlockSpec((height, depth), lambda i: (0, 0), pipeline_mode=pl.Buffered(1)),
            pl.BlockSpec((depth, unit), lambda i: (0, jnp.minimum(first + i, blocks - 1))),
        ],
        grid=(count,),
        out_specs=[pl.BlockSpec((height, unit), lambda i: (i, 0))],
        out_shape=[jax.ShapeDtypeStruct((height * count, unit), BF16)],
        cost_estimate=cost(2 * height * depth * unit * count, 2 * depth * unit * count),
    )[0]


def rotate_pieces(order, pieces, offsets, tokens, basis, lower, width, most):
    depth = basis.shape[0]
    tile = tile_of(math.gcd(width, lower) if lower else width, most)
    first = lower // tile
    count = len(pieces)

    def body(offsets_ref, *refs):
        held, (basis_ref, out_ref, rows_ref, sems) = refs[:count], refs[count:]

        @pl.when(pl.program_id(0) == 0)
        def _():
            copies = []
            for n, piece in enumerate(held):
                size = piece.shape[0]
                where = pl.multiple_of(offsets_ref[n] * size, size)
                copies.append(
                    pltpu.make_async_copy(piece, rows_ref.at[pl.ds(where, size), :], sems.at[n])
                )
            for copy in copies:
                copy.start()
            for copy in copies:
                copy.wait()

        out_ref[...] = jnp.dot(rows_ref[...], basis_ref[...], preferred_element_type=F32).astype(
            BF16
        )

    return order.call(
        body,
        [offsets, *pieces, basis],
        [SMEM] + [ANY] * count + [pl.BlockSpec((depth, tile), lambda i: (0, first + i))],
        grid=(width // tile,),
        out_specs=[pl.BlockSpec((tokens, tile), lambda i: (0, i))],
        out_shape=[jax.ShapeDtypeStruct((tokens, width), BF16)],
        scratch_shapes=[
            pltpu.VMEM((tokens, depth), BF16),
            pltpu.SemaphoreType.DMA((count,)),
        ],
        cost_estimate=cost(2 * tokens * depth * width, 2 * depth * width),
    )[0]


def pick(place, groups):
    result = groups[0][1]
    for places, value in groups[1:]:
        here = functools.reduce(jnp.logical_or, [place == p for p in places])
        result = jnp.where(here, value, result)
    return result


class Line:
    def __init__(self, axis, size, place, shape, count):
        self.axis, self.size, self.place = axis, size, place
        self.shape, self.count = shape, count
        self.parts = []
        self.got = [{}, {}]

    def step(self, order, s):
        size, (rows, columns) = self.size, self.shape
        halves = 2
        block = (rows // halves, columns)
        plan, operands, specs = [], [self.place], [SMEM]
        for parity in (0, 1):
            groups = {}
            for place in range(size):
                if parity == 1 and place in (0, size - 1):
                    continue
                chunk = s - LAG * (place if place % 2 == parity else size - 1 - place)
                if 0 <= chunk < self.count:
                    groups.setdefault(chunk, []).append(place)
            if not groups:
                continue
            for chunk in groups:
                array, row, column = self.parts[chunk]
                operands.append(array)
                specs.append(
                    pl.BlockSpec(block, lambda i, r=row, c=column: (r * halves + i, c))
                )
            before = self.got[1 - parity].get(s - LAG)
            if before is not None:
                operands.append(before)
                specs.append(pl.BlockSpec(block, lambda i: (i, 0)))
            plan.append((parity, list(groups.values()), before is not None))
        outs = len(plan)

        def body(place_ref, *refs):
            place = place_ref[0]
            loads, refs = refs[len(refs) - outs :], iter(refs)
            for (_, groups, more), load in zip(plan, loads):
                value = pick(place, [(places, next(refs)[...]) for places in groups])
                if more:
                    value = (value.astype(F32) + next(refs)[...].astype(F32)).astype(BF16)
                load[...] = value

        loads = order.call(
            body,
            operands,
            specs,
            grid=(halves,),
            out_specs=[pl.BlockSpec(block, lambda i: (i, 0))] * outs,
            out_shape=[jax.ShapeDtypeStruct(self.shape, BF16)] * outs,
            cost_estimate=cost(rows * columns * 4, 2 * rows * columns * (len(operands) + outs)),
        )
        for (parity, _, _), load in zip(plan, loads):
            pairs = []
            for place in range(parity, size - 1, 2):
                pairs += [(place, place + 1), (place + 1, place)]
            self.got[parity][s] = lax.ppermute(load, self.axis, pairs)

    def terms(self, chunk):
        groups = {}
        for place in range(self.size):
            keys = []
            if place > 0:
                keys.append(((place - 1) % 2, place - 1))
            if place < self.size - 1:
                keys.append((place % 2, self.size - 2 - place))
            groups.setdefault(tuple(sorted(keys)), []).append(place)
        return [
            (places, [self.got[parity][chunk + LAG * late] for parity, late in keys])
            for keys, places in groups.items()
        ]


def score(order, line, chunk, query_chunk, query_row, act, qin_turned, eigen, mixed, first, queries):
    tokens, inner = act.shape
    unit = line.shape[1]
    tile = tile_of(unit, 256)
    tiles = unit // tile
    step = tile_of(inner, 256)
    length = tokens // SEQS
    gain = 1.0 / math.sqrt(tokens)
    operands, specs, plan = [line.place], [SMEM], []
    share = line.shape[0] // queries
    for number, row, height in ((chunk, 0, tokens), (query_chunk, query_row, queries)):
        array, low, column = line.parts[number]
        low = low * (share if height == queries else 1) + row
        operands.append(array)
        specs.append(
            pl.BlockSpec((height, tile), lambda i, r=low, c=column: (r, c * tiles + i))
        )
        groups = []
        for places, arrays in line.terms(number):
            for array in arrays:
                operands.append(array)
                specs.append(pl.BlockSpec((height, tile), lambda i, r=row: (r, i)))
            groups.append((places, len(arrays)))
        plan.append(groups)
    operands += [act, qin_turned, eigen]
    specs += [
        pl.BlockSpec((tokens, inner), lambda i: (0, 0)),
        pl.BlockSpec((inner, queries), lambda i: (0, 0)),
        pl.BlockSpec((tile, inner), lambda i: (first * tiles + i, 0)),
    ]
    aliases = {}
    if mixed is not None:
        aliases = {len(operands): 0}
        operands.append(mixed)
        specs.append(ANY)

    def body(place_ref, *refs):
        place = place_ref[0]
        mixed_ref, score_ref, half_ref = refs[-3:]
        refs = iter(refs)
        totals = []
        for groups in plan:
            own = next(refs)[...].astype(F32)
            sums = []
            for places, number in groups:
                values = [next(refs)[...].astype(F32) for _ in range(number)]
                sums.append((places, functools.reduce(jnp.add, values)))
            totals.append((own + pick(place, sums)).astype(BF16))
        act_ref, qin_ref, eigen_ref = next(refs), next(refs), next(refs)
        turned = jnp.transpose(totals[0])
        for lower in range(0, inner, step):
            span = slice(lower, lower + step)
            inverse = 1.0 / eigen_ref[:, span].astype(F32)
            total = None
            for s in range(SEQS):
                rows = slice(s * length, (s + 1) * length)
                grad = jnp.dot(turned[:, rows], act_ref[rows, span], preferred_element_type=F32)
                precond = grad * inverse
                total = precond if total is None else total + precond
                half_ref[s * tile : (s + 1) * tile, span] = precond.astype(BF16)
            mixed_ref[:, span] = (total * gain).astype(BF16)
        projected = jnp.dot(half_ref[...], qin_ref[...], preferred_element_type=F32)
        qout = jnp.transpose(totals[1]).astype(F32)

        @pl.when(pl.program_id(0) == 0)
        def _():
            score_ref[...] = jnp.zeros_like(score_ref)

        for s in range(SEQS):
            part = projected[s * tile : (s + 1) * tile] * qout
            score_ref[s : s + 1, :] += jnp.sum(part, axis=0, keepdims=True)

    return order.call(
        body,
        operands,
        specs,
        grid=(tiles,),
        out_specs=[
            pl.BlockSpec((tile, inner), lambda i: (first * tiles + i, 0)),
            pl.BlockSpec((SEQS, queries), lambda i: (0, 0)),
        ],
        out_shape=[
            jax.ShapeDtypeStruct(eigen.shape, BF16),
            jax.ShapeDtypeStruct((SEQS, queries), F32),
        ],
        scratch_shapes=[pltpu.VMEM((SEQS * tile, inner), BF16)],
        input_output_aliases=aliases,
        cost_estimate=cost(
            2 * unit * inner * (tokens * 2 + SEQS * queries), 4 * unit * inner
        ),
    )


class Gather:
    def __init__(self, own, outs):
        self.own, self.outs = own, outs
        self.index = lax.axis_index("out")
        self.bits = []
        bit = 2
        while bit < outs:
            self.bits.append(bit)
            bit *= 2
        low, high = self.bits[:2]
        self.near = [swap(own, "out", outs, low), swap(own, "out", outs, high)]
        self.pieces = [(own, self.index), self.moved((own, self.index), 1)]

    def moved(self, piece, bit):
        x, offset = piece
        rows = self.own.shape[0]
        return swap(x, "out", self.outs, bit), offset ^ (bit * (rows // x.shape[0]))

    def spread(self, order):
        rows, depth = self.own.shape
        half = rows // 2
        low, high = self.bits[:2]
        one, two = self.near

        def body(one_ref, two_ref, below_ref, above_ref):
            below_ref[...] = one_ref[...]
            above_ref[...] = two_ref[...]

        below, above = order.call(
            body,
            [one, two],
            [
                pl.BlockSpec((half, depth), lambda i: (1, 0)),
                pl.BlockSpec((half, depth), lambda i: (0, 0)),
            ],
            grid=(1,),
            out_specs=[pl.BlockSpec((half, depth), lambda i: (0, 0))] * 2,
            out_shape=[jax.ShapeDtypeStruct((half, depth), BF16)] * 2,
            cost_estimate=cost(half * depth, 8 * half * depth),
        )
        far = (self.index ^ (low | high)) * 2
        late = [
            (one, self.index ^ low),
            (two, self.index ^ high),
            (swap(above, "out", self.outs, low), far),
            (swap(below, "out", self.outs, high), far + 1),
        ]
        self.pieces += late + [self.moved(piece, 1) for piece in late]
        for bit in self.bits[2:]:
            self.pieces += [self.moved(piece, bit) for piece in self.pieces]
        offsets = jnp.stack([offset for _, offset in self.pieces]).astype(jnp.int32)
        return [x for x, _ in self.pieces], offsets


class SumOut:
    def __init__(self, outs, core):
        self.outs, self.core = outs, core
        self.bits = []
        bit = 2
        while bit < outs:
            self.bits.append(bit)
            bit *= 2

    def start(self, order, rows, more, basis, tile):
        (tokens, depth), extra = rows.shape, more.shape[0]
        half = (tokens + extra) // 2
        width = basis.shape[1]

        def body(core_ref, rows_ref, more_ref, basis_ref, keep_ref, give_ref, all_ref):
            @pl.when(pl.program_id(0) == 0)
            def _():
                all_ref[:tokens] = rows_ref[...]
                all_ref[tokens:] = more_ref[...]

            for ref, side in ((keep_ref, core_ref[0]), (give_ref, 1 - core_ref[0])):
                at = pl.multiple_of(side * half, half)
                ref[...] = jnp.dot(
                    all_ref[pl.ds(at, half), :], basis_ref[...], preferred_element_type=F32
                ).astype(ref.dtype)

        self.keep, give = order.call(
            body,
            [self.core, rows, more, basis],
            [
                SMEM,
                pl.BlockSpec((tokens, depth), lambda i: (0, 0)),
                pl.BlockSpec((extra, depth), lambda i: (0, 0)),
                pl.BlockSpec((depth, tile), lambda i: (0, i)),
            ],
            grid=(width // tile,),
            out_specs=[pl.BlockSpec((half, tile), lambda i: (0, i))] * 2,
            out_shape=[
                jax.ShapeDtypeStruct((half, width), F32),
                jax.ShapeDtypeStruct((half, width), BF16),
            ],
            scratch_shapes=[pltpu.VMEM((tokens + extra, depth), BF16)],
            cost_estimate=cost(4 * half * depth * width, 2 * depth * width),
        )
        self.got = swap(give, "out", self.outs, 1)
        self.stage, self.done = 0, False

    def pieces(self):
        half = self.keep.shape[0]
        return half // 2, self.keep.shape[1]

    def advance(self, order):
        piece, width = self.pieces()
        grid = 2
        block = (piece // grid, width)
        done = self.stage == len(self.bits)
        if self.stage == 0:
            operands = [self.keep, self.keep, self.got, self.got]
            specs = [pl.BlockSpec(block, lambda i, n=n: (n * grid + i, 0)) for n in (0, 1, 0, 1)]
        else:
            operands = list(self.held) + list(self.got)
            specs = [pl.BlockSpec(block, lambda i: (i, 0))] * 4

        def body(low, high, low_more, high_more, *outs):
            for n, (a, b) in enumerate(((low, low_more), (high, high_more))):
                value = a[...] + b[...].astype(F32)
                if done:
                    outs[0][n] = value.astype(BF16)
                else:
                    outs[n][...] = value.astype(BF16)
                    outs[2 + n][...] = value

        if done:
            out_specs = [pl.BlockSpec((2,) + block, lambda i: (0, i, 0))]
            out_shape = [jax.ShapeDtypeStruct((2, piece, width), BF16)]
        else:
            out_specs = [pl.BlockSpec(block, lambda i: (i, 0))] * 4
            out_shape = [
                jax.ShapeDtypeStruct((piece, width), kind) for kind in (BF16, BF16, F32, F32)
            ]
        outs = order.call(
            body,
            operands,
            specs,
            grid=(grid,),
            out_specs=out_specs,
            out_shape=out_shape,
            cost_estimate=cost(2 * piece * width, 12 * piece * width),
        )
        if done:
            self.mine = outs[0].reshape(2 * piece, width)
            self.other = swap(self.mine, "out", self.outs, 1)
            self.done = True
            return
        self.held = outs[2:]
        self.got = [
            swap(outs[0], "out", self.outs, self.bits[self.stage]),
            swap(outs[1], "out", self.outs, self.bits[-1 - self.stage]),
        ]
        self.stage += 1

    def finish(self, order, tokens):
        half, width = self.mine.shape
        extra = 2 * half - tokens

        def body(core_ref, mine_ref, other_ref, act_ref, turned_ref):
            first = core_ref[0] == 0
            top = jnp.where(first, mine_ref[...], other_ref[...])
            bottom = jnp.where(first, other_ref[...], mine_ref[...])
            act_ref[:half] = top
            act_ref[half:] = bottom[: tokens - half]
            turned_ref[...] = jnp.transpose(bottom[tokens - half :])

        tile = tile_of(width, 512)
        return order.call(
            body,
            [self.core, self.mine, self.other],
            [SMEM] + [pl.BlockSpec((half, tile), lambda i: (0, i))] * 2,
            grid=(width // tile,),
            out_specs=[
                pl.BlockSpec((tokens, tile), lambda i: (0, i)),
                pl.BlockSpec((tile, extra), lambda i: (i, 0)),
            ],
            out_shape=[
                jax.ShapeDtypeStruct((tokens, width), BF16),
                jax.ShapeDtypeStruct((width, extra), BF16),
            ],
            cost_estimate=cost(2 * half * width, 8 * half * width),
        )


def on_device(
    outs,
    ins,
    activations,
    out_grad,
    basis_out,
    basis_in,
    eigenvalues,
    query_out,
    query_in,
    query_domain,
    seq_weight,
):
    tokens = activations.shape[0] * ins
    queries = query_out.shape[0]
    columns = basis_out.shape[1]
    inner = basis_in.shape[1]
    order = Order()

    act_rows = lax.all_gather(activations, "in", axis=0, tiled=True)
    gather = Gather(out_grad, outs)
    core = (lax.axis_index("out") & 1).astype(jnp.int32).reshape(1)

    unit = tile_of(columns, 512)
    spans = columns // unit
    share = tokens // queries
    ahead = -(-spans // share)
    place = lax.axis_index("in").astype(jnp.int32).reshape(1)
    line = Line("in", ins, place, (tokens, unit), ahead + spans)

    def queries_part(first, count):
        part = rotate_down(order, query_out, basis_out, unit, first * share, count * share)
        line.parts += [(part, c, 0) for c in range(count)]

    def grads_part(first, count):
        part = rotate_pieces(
            order, *gathered, tokens, basis_out, first * unit, count * unit, 256
        )
        line.parts += [(part, 0, c) for c in range(count)]

    mixed, scores = None, []

    def score_part(g):
        nonlocal mixed
        mixed, part = score(
            order,
            line,
            ahead + g,
            g // share,
            g % share,
            rot_act,
            qin_turned,
            eigenvalues,
            mixed,
            g,
            queries,
        )
        scores.append(part)

    late = LAG * (ins - 2)
    last = ahead + spans - 1 + late
    gathered = rot_act = qin_turned = None
    total = SumOut(outs, core)
    plan = {2: 2, 4: 2, 5: spans}
    made = 0
    for s in range(last + 1):
        if s == 0:
            queries_part(0, 1)
        elif made < spans and s >= ahead + made:
            grads_part(made, 1)
            made += 1
        line.step(order, s)
        target = s - 1 - late - ahead
        if s == 0 and ahead > 1:
            queries_part(1, ahead - 1)
        elif s == 1:
            gathered = gather.spread(order)
        elif s == 2:
            total.start(order, act_rows, query_in, basis_in, tile_of(inner, 512))
        while rot_act is None and s >= 3 and (s % 2 == 1 or s > 7 or target >= 0):
            if not total.done:
                total.advance(order)
            else:
                rot_act, qin_turned = total.finish(order, tokens)
            if target < 0:
                break
        count = min(plan.get(s, 0), spans - made)
        if count > 0:
            grads_part(made, count)
            made += count
        if 0 <= target < spans:
            score_part(target)
    while len(scores) < spans:
        score_part(len(scores))

    scores = functools.reduce(jnp.add, scores)
    for axis, size in (("out", outs), ("in", ins)):
        bit = 1
        while bit < size:
            scores = scores + swap(scores, axis, size, bit)
            bit *= 2
    summed = jnp.sum(scores.reshape(SEQS, queries // RANK, RANK), axis=2)
    weights = seq_weight.astype(F32)
    onehot = (query_domain[:, None] == jnp.arange(DOMAINS, dtype=jnp.int32)[None, :]).astype(F32)
    picked = jnp.sum(weights[:, None, :] * onehot[None, :, :], axis=2)
    mean_weight = jnp.sum(weights, axis=1, keepdims=True) / DOMAINS
    return (mixed, summed * picked / mean_weight)


def solution(mesh):
    return jax.shard_map(
        functools.partial(on_device, mesh.shape["out"], mesh.shape["in"]),
        mesh=mesh,
        in_specs=(
            P("in", "out"),
            P("out", "in"),
            P("in", "out"),
            P("out", "in"),
            P("out", "in"),
            P(None, "in"),
            P(None, "out"),
            P(),
            P(),
        ),
        out_specs=(P("out", "in"), P()),
        check_vma=False,
    )
```
